256 devices in a mesh: dp: 16 (over z_lo, x), tensor: 16 (over y, z_hi, core).
Axes of the slice: x: 4, y: 4, z: 8 (z_hi: 2, z_lo: 4; z = z_hi * 4 + z_lo), core: 2. Of those that a mesh axis runs over, the one named last changes fastest.
Arguments:
- layer_in: bfloat16 [16384, 6144], P(('dp', 'tensor')), may hold values from -100 to 100
- out_grad: bfloat16 [16384, 6144], P(('dp', 'tensor')), may hold values from -100 to 100
- gate_pre: bfloat16 [16384, 14336], P('dp', 'tensor'), may hold values from -6 to 6
- up_pre: bfloat16 [16384, 14336], P('dp', 'tensor'), may hold values from -6 to 6
- down_weight: bfloat16 [14336, 6144], P('tensor', 'dp'), may hold values from -0.078125 to 0.078125
- proj_in: bfloat16 [6144, 64], replicated, may hold values from -0.078125 to 0.078125
- proj_gate: bfloat16 [14336, 64], P('tensor'), may hold values from -0.046875 to 0.046875
- proj_up: bfloat16 [14336, 64], P('tensor'), may hold values from -0.046875 to 0.046875
- eval_sketch: bfloat16 [512, 8192], P('dp'), may hold values from -6 to 6
Outputs:
- scores: float32 [16, 512], P('dp')
The draws below stay inside these ranges and needn't reach their ends.
All inputs are finite; a program needn't handle non-finite values.
Results may differ from the reference program's by a relative error of at most 0.0031.
Values may be sent and summed in bfloat16 or wider, within the bound.
No kernel may reach another device: no remote copies, remote signals or barrier semaphores. Data moves between devices by JAX's collectives and lax.ppermute only.
A program may use at most 128 MiB of HBM per device.

```python
import math
import jax
import jax.numpy as jnp
from jax import lax

D = 6144
FF = 14336
R = 64
SEQS = 1
SEQ_LEN = 1024
TOKENS = 16384
EVAL = 512


def activation_field(key, noise_draw, row_top, rise):
    key_row, key_col = jax.random.split(key, 2)
    row_count, col_count = noise_draw.shape
    row_scale = jnp.exp(jax.random.uniform(key_row, (row_count, 1), jnp.float32) * math.log(row_top))
    col_scale = jnp.exp(jax.random.uniform(key_col, (1, col_count), jnp.float32) * math.log(10.0))
    group_rows = SEQS * SEQ_LEN
    last_group = max(row_count // group_rows - 1, 1)
    group_index = (jnp.arange(row_count, dtype=jnp.int32) // group_rows).astype(jnp.float32)[:, None]
    rise_factor = 1.0 + (rise - 1.0) * group_index / last_group
    return noise_draw * row_scale * col_scale * rise_factor * 0.1


def draw_layer_in(key, part):
    key = jax.random.fold_in(key, 1)
    key_noise, key_field = jax.random.split(key)
    noise_draw = jnp.clip(jax.random.normal(key_noise, (TOKENS, D), jnp.float32), -4.0, 4.0)
    return activation_field(key_field, noise_draw, 10.0, 1.732).astype(jnp.bfloat16)


def draw_out_grad(key, part):
    key = jax.random.fold_in(key, 2)
    key_noise, key_field = jax.random.split(key)
    noise_draw = jnp.clip(jax.random.normal(key_noise, (TOKENS, D), jnp.float32), -4.0, 4.0)
    return activation_field(key_field, noise_draw, 10.0, 1.732).astype(jnp.bfloat16)


def shard_levels(rng, dims, cuts, smallest, high):
    def one(axis_at, shards_of):
        heights = jax.random.uniform(jax.random.fold_in(jax.random.fold_in(rng, 6), axis_at), (shards_of,), jnp.float32, smallest / len(cuts), high / len(cuts))
        return jnp.repeat(jnp.exp(heights), dims[axis_at] // shards_of).reshape((-1,) + (1,) * (len(dims) - axis_at - 1))

    loudness = one(*cuts[0])
    for cut in cuts[1:]:
        loudness = loudness * one(*cut)
    return loudness


def normal_values(key, extent, deviation, limit, shards=(), held_as=jnp.bfloat16):
    loudness = shard_levels(key, extent, shards, -0.22, 0.18) if shards else 1.0
    array = jax.random.normal(key, extent, jnp.float32) * deviation * loudness
    return jnp.minimum(jnp.maximum(array, -limit), limit).astype(held_as)


def setup_inputs(seed: int = 0) -> dict:
    arg_keys = jax.random.split(jax.random.key(seed), 10)
    layer_in = draw_layer_in(jax.random.fold_in(arg_keys[9], 71), 0)
    out_grad = draw_out_grad(jax.random.fold_in(arg_keys[9], 71), 0)
    gate_pre = normal_values(arg_keys[2], (TOKENS, FF), 1.0, 6.0, ((0, 16), (1, 16)))
    up_pre = normal_values(arg_keys[3], (TOKENS, FF), 1.0, 6.0, ((0, 16), (1, 16)))
    down_weight = normal_values(arg_keys[4], (FF, D), D ** -0.5, 0.078125, ((0, 16), (1, 16)))
    proj_in = normal_values(arg_keys[5], (D, R), D ** -0.5, 0.078125)
    proj_gate = normal_values(arg_keys[6], (FF, R), FF ** -0.5, 0.046875, ((0, 16),))
    proj_up = normal_values(arg_keys[7], (FF, R), FF ** -0.5, 0.046875, ((0, 16),))
    eval_sketch = normal_values(arg_keys[8], (EVAL, 2 * R * R), 1.0, 6.0, ((0, 16),))
    return {"layer_in": layer_in, "out_grad": out_grad, "gate_pre": gate_pre, "up_pre": up_pre, "down_weight": down_weight, "proj_in": proj_in, "proj_gate": proj_gate, "proj_up": proj_up, "eval_sketch": eval_sketch}


def precondition(covariance, sketches):
    order = covariance.shape[-1]
    identity = jnp.eye(order, dtype=jnp.float32)
    trace_sum = jnp.trace(covariance, axis1=1, axis2=2)
    damping = 0.1 * trace_sum / order + 1e-06
    factors = jnp.linalg.cholesky(covariance + damping[:, None, None] * identity)
    sample_count = sketches.shape[0]
    stacked = jnp.transpose(sketches, (2, 0, 1, 3)).reshape(order, sample_count * 2 * order)
    left_solved = jax.scipy.linalg.cho_solve((factors[0], True), stacked).reshape(order, sample_count, 2, order)
    outcome = []
    for module in range(2):
        flipped = jnp.transpose(left_solved[:, :, module, :], (2, 1, 0)).reshape(order, sample_count * order)
        solved = jax.scipy.linalg.cho_solve((factors[module + 1], True), flipped).reshape(order, sample_count, order)
        outcome.append(jnp.transpose(solved, (1, 2, 0)))
    return jnp.stack(outcome, axis=1)

def reference(layer_in, out_grad, gate_pre, up_pre, down_weight, proj_in, proj_gate, proj_up, eval_sketch):
    highest = lax.Precision.HIGHEST
    group_rows = SEQS * SEQ_LEN
    group_count = layer_in.shape[0] // group_rows
    order = proj_in.shape[1]

    def group_terms(group_index):
        offset = (group_index * group_rows).astype(jnp.int32)
        grad_rows = lax.dynamic_slice_in_dim(out_grad, offset, group_rows, 0)
        gate_val = lax.dynamic_slice_in_dim(gate_pre, offset, group_rows, 0).astype(jnp.float32)
        up_val = lax.dynamic_slice_in_dim(up_pre, offset, group_rows, 0).astype(jnp.float32)
        hidden_grad = lax.dot_general(grad_rows.astype(jnp.float32), down_weight.astype(jnp.float32), (((1,), (1,)), ((), ())), preferred_element_type=jnp.float32)
        sigmoid_gate = jax.nn.sigmoid(gate_val)
        gate_grad = (hidden_grad * up_val * sigmoid_gate * (1.0 + gate_val * (1.0 - sigmoid_gate))).astype(jnp.bfloat16)
        up_grad = (hidden_grad * gate_val * sigmoid_gate).astype(jnp.bfloat16)
        return (jnp.dot(gate_grad.astype(jnp.float32), proj_gate.astype(jnp.float32), preferred_element_type=jnp.float32), jnp.dot(up_grad.astype(jnp.float32), proj_up.astype(jnp.float32), preferred_element_type=jnp.float32))
    gate_proj, up_proj = lax.map(group_terms, jnp.arange(group_count, dtype=jnp.int32))
    gate_proj = gate_proj.reshape(-1, order)
    up_proj = up_proj.reshape(-1, order)
    in_proj = jnp.dot(layer_in.astype(jnp.float32), proj_in.astype(jnp.float32), preferred_element_type=jnp.float32)
    total_rows = layer_in.shape[0]
    moments = jnp.stack([jnp.dot(in_proj.T, in_proj, precision=highest), jnp.dot(gate_proj.T, gate_proj, precision=highest), jnp.dot(up_proj.T, up_proj, precision=highest)]) / total_rows
    seq_in = in_proj.reshape(-1, SEQ_LEN, order)
    sketches = jnp.stack([jnp.einsum('slr,slq->srq', seq_in, gate_proj.reshape(-1, SEQ_LEN, order), precision=highest), jnp.einsum('slr,slq->srq', seq_in, up_proj.reshape(-1, SEQ_LEN, order), precision=highest)], axis=1)
    conditioned = precondition(moments, sketches)
    flat_sketch = conditioned.reshape(sketches.shape[0], -1)
    score_scale = 1.0 / (order * math.sqrt(2.0 * SEQ_LEN))
    eval_wide = eval_sketch.astype(jnp.float32)
    return jnp.dot(flat_sketch, eval_wide.T, precision=highest) * score_scale
```

```python
import math

import jax
import jax.numpy as jnp
from jax import lax
from jax.experimental import pallas as pl
from jax.sharding import Mesh, PartitionSpec as P

SEQ_LEN = 1024
TOKENS = 16384
ORDER = 64
HIGHEST = lax.Precision.HIGHEST
F32 = jnp.float32

RING = (0, -1, 1, 2)


def shift(size, by):
    return [(i, (i + by) % size) for i in range(size)]


def swap(size, bit):
    return [(i, i ^ bit) for i in range(size)]


CROSS = [(0, 3), (3, 0), (1, 2), (2, 1)]


def add_over(value, axis, *perms):
    for perm in perms:
        value = value + lax.ppermute(value, axis, perm)
    return value


def ring_gather(own, axis):
    half = (own.shape[0] // 2) // 16 * 16
    left = lax.ppermute(own, axis, shift(4, 1))
    right = lax.ppermute(own, axis, shift(4, -1))
    top = lax.ppermute(left[:half], axis, shift(4, 1))
    bottom = lax.ppermute(right[half:], axis, shift(4, -1))
    return own, left, right, jnp.concatenate([top, bottom], axis=0)


def solve_kernel(q_ref, o_ref):
    a = q_ref[...]
    row = lax.broadcasted_iota(jnp.int32, a.shape, 0)
    col = lax.broadcasted_iota(jnp.int32, a.shape, 1)
    a = jnp.where(col < ORDER, a * (1.0 / TOKENS), a)
    diag = row == col
    damping = 0.1 * jnp.sum(jnp.where(diag, a, 0.0)) / ORDER + 1e-06
    a = a + jnp.where(diag, damping, 0.0)
    for k in range(ORDER):
        pivot = a[k : k + 1, :] * (1.0 / a[k : k + 1, k : k + 1])
        a = jnp.where(row == k, pivot, a - a[:, k : k + 1] * pivot)
    o_ref[...] = a


def solve(q):
    return pl.pallas_call(solve_kernel, out_shape=jax.ShapeDtypeStruct(q.shape, F32))(q)[:, ORDER:]


def per_device(
    layer_in, out_grad, gate_pre, up_pre, down_weight, proj_in, proj_gate, proj_up, eval_sketch
):
    zl, x, y, zh, c = (lax.axis_index(a) for a in ("zl", "x", "y", "zh", "c"))
    width = down_weight.shape[1]
    rows = out_grad.shape[0]

    def block(r, dx):
        at = ((zl - r) % 4 * 4 + (x + dx) % 4) * width
        return lax.dynamic_slice_in_dim(out_grad, at, width, 1)

    grad_own = jnp.concatenate([block(r, dx) for r in range(4) for dx in RING], axis=1)

    part = 2 * ORDER * ORDER // 16
    evals = lax.dynamic_slice_in_dim(eval_sketch, (c * 8 + y * 2 + zh) * part, part, 1)
    tail = evals.reshape(128, 128)
    tail = jnp.pad(tail, ((0, 16), (0, 0)))
    tail = jnp.concatenate([tail[0:48], tail[48:96], tail[96:144]], axis=1)
    load = jnp.concatenate([down_weight, tail], axis=0)

    hidden = down_weight.shape[0]
    slabs = [load]
    for r in range(3):
        slabs.append(lax.ppermute(slabs[-1], "zl", shift(4, 1)))
    slabs = [ring_gather(s, "x") for s in slabs]

    grad_far = lax.ppermute(grad_own, "zh", swap(2, 1))
    mine = [jnp.concatenate(ring_gather(s, "y"), axis=0) for s in (grad_own, grad_far)]
    theirs = [lax.ppermute(s, "c", swap(2, 1)) for s in mine]

    def rows_of(array, dzh, dc):
        at = [((((y + dy) % 4) * 2 + (zh ^ dzh)) * 2 + (c ^ dc)) * rows for dy in RING]
        return jnp.concatenate([lax.dynamic_slice_in_dim(array, a, rows, 0) for a in at], axis=0)

    in_proj = jnp.dot(layer_in, proj_in, preferred_element_type=F32)
    in_moment = lax.dot_general(in_proj, in_proj, (((0,), (0,)), ((), ())), precision=HIGHEST)
    in_moment = add_over(in_moment, "c", swap(2, 1))
    in_moment = add_over(in_moment, "zh", swap(2, 1))
    in_moment = add_over(in_moment, "y", swap(4, 1), CROSS)
    in_moment = add_over(in_moment, "x", swap(4, 1), CROSS)
    in_moment = add_over(in_moment, "zl", swap(4, 1), swap(4, 2))
    in_solved = solve(jnp.concatenate([in_moment, in_proj.T], axis=1)).T

    weights = [jnp.concatenate([p[:hidden] for p in s], axis=1) for s in slabs]
    depth = 4 * width

    def group(grad, dzh, dc):
        hidden_grad = sum(
            lax.dot_general(
                grad[:, r * depth : (r + 1) * depth],
                weights[r],
                (((1,), (1,)), ((), ())),
                preferred_element_type=F32,
            )
            for r in range(4)
        )
        gate_val = rows_of(gate_pre, dzh, dc).astype(F32)
        up_val = rows_of(up_pre, dzh, dc).astype(F32)
        sig = jax.nn.sigmoid(gate_val)
        gate_grad = (hidden_grad * up_val * sig * (1.0 + gate_val * (1.0 - sig))).astype(jnp.bfloat16)
        up_grad = (hidden_grad * gate_val * sig).astype(jnp.bfloat16)
        return jnp.concatenate(
            [
                jnp.dot(gate_grad, proj_gate, preferred_element_type=F32),
                jnp.dot(up_grad, proj_up, preferred_element_type=F32),
            ],
            axis=1,
        )

    kept = jnp.concatenate([group(mine[0], 0, 0), group(mine[1], 1, 0)], axis=0)
    sent = jnp.concatenate([group(theirs[0], 0, 1), group(theirs[1], 1, 1)], axis=0)
    kept = kept + lax.ppermute(sent, "c", swap(2, 1))
    half = kept.shape[0] // 2
    kept = kept[:half] + lax.ppermute(kept[half:], "zh", swap(2, 1))
    proj = kept[:rows]
    for i, dy in enumerate(RING[1:], 1):
        proj = proj + lax.ppermute(kept[i * rows : (i + 1) * rows], "y", shift(4, dy))

    def sides(module):
        both = jnp.concatenate([module, in_solved], axis=1)
        return lax.dot_general(module, both, (((0,), (0,)), ((), ())), precision=HIGHEST)

    gate_q, up_q = sides(proj[:, :ORDER]), sides(proj[:, ORDER:])
    q = jnp.where(c == 0, gate_q, up_q) + lax.ppermute(
        jnp.where(c == 0, up_q, gate_q), "c", swap(2, 1)
    )
    q = add_over(q, "zh", swap(2, 1))
    q = add_over(q, "y", swap(4, 1), CROSS)
    moment = add_over(q[:, :ORDER], "x", swap(4, 1), CROSS)
    moment = add_over(moment, "zl", swap(4, 1), swap(4, 2))
    solved = solve(jnp.concatenate([moment, q[:, ORDER:]], axis=1)).T

    def unpack(piece):
        t = piece[hidden:]
        t = jnp.concatenate([t[:, 0:128], t[:, 128:256], t[:32, 256:384]], axis=0)
        return t.reshape(1, 1, 32, part)

    held = [slabs[r] for r in (0, 3, 2, 1)]
    held = jnp.concatenate(
        [jnp.concatenate([unpack(s[i]) for i in (0, 2, 3, 1)], axis=1) for s in held], axis=0
    )
    held = lax.dynamic_slice_in_dim(jnp.concatenate([held, held], axis=0), (4 - zl) % 4, 4, 0)
    held = lax.dynamic_slice_in_dim(jnp.concatenate([held, held], axis=1), (4 - x) % 4, 4, 1)
    held = held.reshape(-1, part)

    mine_rows = lax.dynamic_slice_in_dim(solved, (y * 2 + zh) * 8, 8, 0).reshape(1, part)
    scores = lax.dot_general(
        mine_rows, held.astype(F32), (((1,), (1,)), ((), ())), precision=HIGHEST
    ) * (1.0 / (ORDER * math.sqrt(2.0 * SEQ_LEN)))
    scores = add_over(scores, "c", swap(2, 1))
    scores = add_over(scores, "zh", swap(2, 1))
    return add_over(scores, "y", swap(4, 1), CROSS)


def solution(mesh):
    fine = Mesh(mesh.devices.reshape(4, 4, 4, 2, 2), ("zl", "x", "y", "zh", "c"))
    dp, tensor = ("zl", "x"), ("y", "zh", "c")
    placed = (
        P(dp + tensor, None),
        P(dp + tensor, None),
        P(dp, tensor),
        P(dp, tensor),
        P(tensor, dp),
        P(),
        P(tensor, None),
        P(tensor, None),
        P(dp, None),
    )
    return jax.shard_map(
        per_device, mesh=fine, in_specs=placed, out_specs=P(dp, None), check_vma=False
    )
```

```python
import functools
import math

import jax
import jax.numpy as jnp
from jax import lax
from jax.experimental import pallas as pl
from jax.experimental.pallas import tpu as pltpu
from jax.sharding import Mesh, PartitionSpec as P

SEQ_LEN = 1024
TOKENS = 16384
ORDER = 64
HIGHEST = lax.Precision.HIGHEST
F32 = jnp.float32
BF16 = jnp.bfloat16
ANY = pl.BlockSpec(memory_space=pl.ANY)
SMEM = pl.BlockSpec(memory_space=pltpu.SMEM)
VMEM = pl.BlockSpec(memory_space=pltpu.VMEM)
PARAMS = pltpu.CompilerParams(vmem_limit_bytes=14 * 1024 * 1024)
TAIL = 48
NT = (((1,), (1,)), ((), ()))


def swap(size, bit):
    return [(i, i ^ bit) for i in range(size)]


CROSS = [(0, 3), (3, 0), (1, 2), (2, 1)]


def opposed(by):
    return [(i * 2 + k, (i + (by if k == 0 else -by)) % 4 * 2 + k) for i in range(4) for k in range(2)]


def add_over(value, axis, *perms):
    for perm in perms:
        value = value + lax.ppermute(value, axis, perm)
    return value


def after(value, *gates):
    return lax.optimization_barrier((value, *gates))[0] if gates else value


def ring_gather(own, axis):
    held = [own]
    for _ in range(3):
        held.append(lax.ppermute(held[-1], (axis, "c"), opposed(1)))
    return held


def load_kernel(at, weight, evals, out, sems):
    n = weight.shape[0]
    column = pl.multiple_of(at[5], 128)
    copies = [pltpu.make_async_copy(weight, out.at[pl.ds(0, n)], sems.at[0])]
    for i in range(3):
        copies.append(
            pltpu.make_async_copy(
                evals.at[:, pl.ds(column + i * 128, 128)],
                out.at[pl.ds(n, 32), pl.ds(i * 128, 128)],
                sems.at[i + 1],
            )
        )
    for i in range(2):
        copies.append(
            pltpu.make_async_copy(
                evals.at[pl.ds(i * 16, 16), pl.ds(column + 384, 128)],
                out.at[pl.ds(n + 32, 16), pl.ds(i * 128, 128)],
                sems.at[i + 4],
            )
        )
    for copy in copies:
        copy.start()
    for copy in copies:
        copy.wait()


def unload(at, units, pieces, out):
    n = pieces[0].shape[0] - TAIL
    zl, x, c = at[0], at[1], at[4]
    for (s, i), piece in zip(units, pieces):
        row = pl.multiple_of(((zl + 4 - s) % 4 * 4 + (x + 4 + i * (2 * c - 1)) % 4) * 32, 32)
        out[pl.ds(row, 32), 0:384] = piece[n : n + 32, :]
        out[pl.ds(row, 16), 384:512] = piece[n + 32 :, 0:128]
        out[pl.ds(row + 16, 16), 384:512] = piece[n + 32 :, 128:256]


def unit_terms(at, units, weights, grads):
    width = weights[0].shape[1]
    hidden = weights[0].shape[0] - TAIL
    for (s, i), weight in zip(units, weights):
        block = (at[0] + 4 - s) % 4 * 4 + (at[1] + 4 + i * (2 * at[4] - 1)) % 4
        columns = pl.ds(pl.multiple_of(block * width, width), width)
        rows = jnp.concatenate([p[:, columns] for p in grads], axis=0)
        yield lax.dot_general(rows, weight[:hidden, :], NT, preferred_element_type=F32)


def add_kernel(units, first, at, *refs):
    n = len(units)
    weights, grads, out = refs[:n], refs[n : n + 8], refs[-1]
    total = None if first else refs[n + 8][...]
    for term in unit_terms(at, units, weights, grads):
        total = term if total is None else total + term
    out[...] = total


def add_units(name, at, units, slabs, grads, acc=None):
    n = len(units)
    hidden, width = slabs[0][0].shape[0] - TAIL, slabs[0][0].shape[1]
    operands = [at] + [slabs[s][i] for s, i in units] + list(grads) + ([] if acc is None else [acc])
    return pl.pallas_call(
        functools.partial(add_kernel, units, acc is None),
        out_shape=jax.ShapeDtypeStruct((512, hidden), F32),
        in_specs=[SMEM] + [VMEM] * (len(operands) - 1),
        out_specs=VMEM,
        compiler_params=PARAMS,
        cost_estimate=pl.CostEstimate(flops=2 * 512 * hidden * n * width, bytes_accessed=5_000_000, transcendentals=0),
        name=name,
    )(*operands)


def unload_kernel(units, at, *refs):
    unload(at, units, refs[:-1], refs[-1])


def last_kernel(units, at, *refs):
    n = len(units)
    weights, refs = refs[:n], refs[n:]
    halves, refs = (refs[:8], refs[8:16]), refs[16:]
    accs, (gate_pre, up_pre, proj_gate, proj_up, evals_in, out, evals) = refs[:2], refs[2:]
    evals[...] = evals_in[...]
    unload(at, units, weights, evals)
    y, zh, c = at[2], at[3], at[4]
    for g in range(4):
        dzh, dc = g // 2, g % 2
        core = c ^ dc
        blocks = [((y + 4 + i * (2 * core - 1)) % 4) * 2 + (zh ^ dzh) for i in range(4)]

        def recorded(ref):
            at_rows = [pl.multiple_of((block * 2 + core) * 64, 64) for block in blocks]
            return jnp.concatenate([ref[pl.ds(r, 64), :] for r in at_rows], axis=0).astype(F32)

        total = accs[dzh][dc * 256 : (dc + 1) * 256, :]
        for term in unit_terms(at, units, weights, halves[dzh][dc * 4 : (dc + 1) * 4]):
            total = total + term
        gate_val, up_val = recorded(gate_pre), recorded(up_pre)
        sig = jax.nn.sigmoid(gate_val)
        gate_grad = (total * up_val * sig * (1.0 + gate_val * (1.0 - sig))).astype(BF16)
        up_grad = (total * gate_val * sig).astype(BF16)
        result = jnp.concatenate(
            [
                lax.dot_general(gate_grad, proj_gate[...], NT, preferred_element_type=F32),
                lax.dot_general(up_grad, proj_up[...], NT, preferred_element_type=F32),
            ],
            axis=1,
        )
        for i, block in enumerate(blocks):
            out[pl.ds(pl.multiple_of(dc * 512 + block * 64, 64), 64), :] = result[i * 64 : (i + 1) * 64, :]


def last_units(at, units, slabs, own, far, acc_own, acc_far, pres, projs, evals):
    operands = [at] + [slabs[s][i] for s, i in units] + [*own, *far, acc_own, acc_far, *pres, *projs, evals]
    return pl.pallas_call(
        functools.partial(last_kernel, units),
        out_shape=(jax.ShapeDtypeStruct((SEQ_LEN, 2 * ORDER), F32), jax.ShapeDtypeStruct(evals.shape, BF16)),
        in_specs=[SMEM] + [VMEM] * (len(operands) - 1),
        out_specs=(VMEM, VMEM),
        compiler_params=PARAMS,
        name="last",
    )(*operands)


def product_kernel(at, blocks, in_proj, keep, send):
    proj = sum(blocks[i] for i in range(8))
    z = jnp.concatenate([proj, in_proj[...]], axis=1)
    g = lax.dot_general(z, z, (((0,), (0,)), ((), ())), precision=HIGHEST, preferred_element_type=F32)
    n = ORDER
    row = lax.broadcasted_iota(jnp.int32, (n, n), 0)
    col = lax.broadcasted_iota(jnp.int32, (n, n), 1)
    in_moment = g[2 * n :, 2 * n :]
    in_diag = jnp.sum(jnp.where(row == col, in_moment, 0.0), axis=0, keepdims=True)
    in_diag = jnp.concatenate([jnp.broadcast_to(in_diag, (8, n))] * 2, axis=1)

    def pack(m):
        side = g[m * n : (m + 1) * n, 2 * n :]
        both = jnp.where(row < col, in_moment, g[m * n : (m + 1) * n, m * n : (m + 1) * n])
        halves = [jnp.concatenate([v[: n // 2], v[n // 2 :]], axis=1) for v in (both, side)]
        return jnp.concatenate([halves[0], in_diag, halves[1]], axis=0)

    gate, up = pack(0), pack(1)
    keep[...] = jnp.where(at[4] == 0, gate, up)
    send[...] = jnp.where(at[4] == 0, up, gate)


def score_kernel(at, moments, side, evals, out, inverse):
    n = ORDER
    packed = sum(moments[i] for i in range(16))
    both = jnp.concatenate([packed[: n // 2, :n], packed[: n // 2, n:]], axis=0)
    in_diag = packed[n // 2 : n // 2 + 1, :n]
    row = lax.broadcasted_iota(jnp.int32, (n, 2 * n), 0)
    col = lax.broadcasted_iota(jnp.int32, (n, 2 * n), 1)
    diag = row == col
    lower = (row >= col)[:, :n]
    mirrored = both.T
    moment = jnp.where(lower, both, mirrored)
    in_moment = jnp.where(lower, mirrored, both)
    in_moment = jnp.where(diag[:, :n], jnp.broadcast_to(in_diag, (n, n)), in_moment)
    right = jnp.concatenate([side[:, :n], side[:, n:]], axis=0)
    eye = jnp.where(diag, 1.0, 0.0)[:, :n]

    def damped(m, rhs):
        a = jnp.concatenate([m * (1.0 / TOKENS), rhs], axis=1)
        damping = 0.1 * jnp.sum(jnp.where(diag, a, 0.0)) / n + 1e-06
        return a + jnp.where(diag, damping, 0.0)

    def spread(a, k):
        return [jnp.broadcast_to(a[:, k + j : k + j + 1], a.shape) for j in range(8)]

    def pivot(a, cols, k, j):
        at_row = row == k + j
        inv = 1.0 / cols[j][k + j : k + j + 1, :]

        def eliminate(m):
            scaled = m[k + j : k + j + 1, :] * inv
            return jnp.where(at_row, scaled, m - cols[j] * scaled)

        return eliminate(a), [m if i <= j else eliminate(m) for i, m in enumerate(cols)]

    a0 = damped(in_moment, eye)
    a1 = damped(moment, right)
    for k in range(0, n, 8):
        c0, c1 = spread(a0, k), spread(a1, k)
        for j in range(8):
            a0, c0 = pivot(a0, c0, k, j)
            a1, c1 = pivot(a1, c1, k, j)
    inverse[...] = a0[:, n:]
    mine = inverse[pl.ds(pl.multiple_of((at[2] * 2 + at[3]) * 8, 8), 8), :]
    part = lax.dot_general(
        mine, a1[:, n:], (((1,), (1,)), ((), ())), precision=HIGHEST, preferred_element_type=F32
    ) * (1.0 / (n * math.sqrt(2.0 * SEQ_LEN)))
    flat = jnp.concatenate([part[i : i + 1, :] for i in range(8)], axis=1)
    high = flat.astype(BF16)
    rest = flat - high.astype(F32)
    mid = rest.astype(BF16)
    low = (rest - mid.astype(F32)).astype(BF16)
    three = jnp.concatenate([high, mid, low], axis=0)
    scores = lax.dot_general(three, evals[...], (((1,), (1,)), ((), ())), preferred_element_type=F32)
    out[...] = scores[0:1] + scores[1:2] + scores[2:3]


def per_device(
    layer_in, out_grad, gate_pre, up_pre, down_weight, proj_in, proj_gate, proj_up, eval_sketch
):
    zl, x, y, zh, c = (lax.axis_index(a) for a in ("zl", "x", "y", "zh", "c"))
    part = 2 * ORDER * ORDER // 16
    at = jnp.stack([zl, x, y, zh, c, (c * 8 + y * 2 + zh) * part]).astype(jnp.int32)
    hidden, width = down_weight.shape
    rows = out_grad.shape[0]
    core = swap(2, 1)

    load = pl.pallas_call(
        load_kernel,
        out_shape=jax.ShapeDtypeStruct((hidden + TAIL, width), BF16),
        in_specs=[SMEM, ANY, ANY],
        out_specs=VMEM,
        scratch_shapes=[pltpu.SemaphoreType.DMA((6,))],
        compiler_params=PARAMS,
        name="load",
    )(at, down_weight, eval_sketch)

    def along_z(value, *gates):
        return lax.ppermute(after(value, *gates), "zl", [(i, (i + 1) % 4) for i in range(4)])

    def over_z(value, *gates):
        return lax.ppermute(after(value, *gates), "zh", core)

    def along_x(n, s):
        slabs[s].append(lax.ppermute(after(slabs[s][-1], *steps[-2:-1], *hold), ("x", "c"), opposed(1)))
        steps.append(slabs[s][-1])

    def other_core(pieces, gate):
        return [lax.ppermute(after(p, gate), "c", core) for p in pieces]

    def origins(dcs, dzh, start):
        return [(dc, dzh, i, start) for dc in dcs for i in range(4)]

    gates = []

    def along(axis, held, *more):
        held.append(lax.ppermute(after(held[-1], *more), (axis, "c"), opposed(1)))

    def other_core(pieces, *more):
        return [lax.ppermute(after(p, *more), "c", core) for p in pieces]

    def along_z(value, *more):
        return lax.ppermute(after(value, *more), "zl", [(i, (i + 1) % 4) for i in range(4)])

    slabs, own = [[load]], [out_grad]
    slabs.append([along_z(load)])
    slabs.append([along_z(slabs[1][0])])
    far = [lax.ppermute(after(out_grad, slabs[2][0]), "zh", core)]
    slabs.append([along_z(slabs[2][0], far[0])])
    for _ in range(3):
        along("x", slabs[0])
        along("y", own)
    for _ in range(3):
        along("x", slabs[1])
        along("x", slabs[2])
    for _ in range(3):
        along("y", far, own[3])
    own = own + other_core(own, own[3])
    far = far + other_core(far[:2], far[2]) + other_core(far[2:], far[3])
    units = [(s, i) for s in (0, 1) for i in range(4)]
    acc_own = add_units("own0", at, units, slabs, own)
    in_proj = jnp.dot(after(layer_in, slabs[1][2]), proj_in, preferred_element_type=F32)
    along("x", slabs[3], acc_own, in_proj)
    more = [(2, i) for i in range(4)] + [(3, 0)]
    units += more
    acc_own = add_units("own1", at, more, slabs, own, acc_own)
    along("x", slabs[3], acc_own)
    units += [(3, 1)]
    acc_own = add_units("own2", at, [(3, 1)], slabs, own, acc_own)
    along("x", slabs[3], acc_own)
    evals = pl.pallas_call(
        functools.partial(unload_kernel, units),
        out_shape=jax.ShapeDtypeStruct((512, part), BF16),
        in_specs=[SMEM] + [VMEM] * len(units),
        out_specs=VMEM,
        compiler_params=PARAMS,
        name="unload",
    )(at, *(slabs[s][i] for s, i in units))
    acc_far = add_units("far", at, units, slabs, far)
    parts, evals = last_units(
        at,
        [(3, 2), (3, 3)],
        slabs,
        own,
        far,
        acc_own,
        acc_far,
        (gate_pre, up_pre),
        (proj_gate.T, proj_up.T),
        evals,
    )

    middle = SEQ_LEN // 2
    kept = parts[:middle] + lax.ppermute(parts[middle:], "c", core)
    blocks = lax.all_to_all(kept.reshape(8, rows, 2 * ORDER), ("y", "zh"), 0, 0)
    packed = ORDER // 2 + 8
    shape = jax.ShapeDtypeStruct((packed + ORDER // 2, 2 * ORDER), F32)
    keep, send = pl.pallas_call(
        product_kernel,
        out_shape=(shape, shape),
        in_specs=[SMEM] + [VMEM] * 2,
        out_specs=(VMEM, VMEM),
        name="product",
    )(at, blocks, in_proj)
    q = keep + lax.ppermute(send, "c", core)
    q = jnp.sum(lax.all_to_all(jnp.broadcast_to(q, (8, *q.shape)), ("y", "zh"), 0, 0), axis=0)
    moments = q[:packed]
    moments = lax.all_to_all(jnp.broadcast_to(moments, (16, *moments.shape)), ("zl", "x"), 0, 0)
    scores = pl.pallas_call(
        score_kernel,
        out_shape=jax.ShapeDtypeStruct((1, 512), F32),
        in_specs=[SMEM] + [VMEM] * 3,
        out_specs=VMEM,
        scratch_shapes=[pltpu.VMEM((ORDER, ORDER), F32)],
        compiler_params=PARAMS,
        name="score",
    )(at, moments, q[packed:], evals)
    scores = lax.all_to_all(jnp.broadcast_to(scores, (16, *scores.shape)), ("y", "zh", "c"), 0, 0)
    return jnp.sum(scores, axis=0)


def solution(mesh):
    fine = Mesh(mesh.devices.reshape(4, 4, 4, 2, 2), ("zl", "x", "y", "zh", "c"))
    dp, tensor = ("zl", "x"), ("y", "zh", "c")
    placed = (
        P(dp + tensor, None),
        P(dp + tensor, None),
        P(dp, tensor),
        P(dp, tensor),
        P(tensor, dp),
        P(),
        P(tensor, None),
        P(tensor, None),
        P(dp, None),
    )
    return jax.shard_map(
        per_device, mesh=fine, in_specs=placed, out_specs=P(dp, None), check_vma=False
    )
```

```python
import functools
import math

import jax
import jax.numpy as jnp
from jax import lax
from jax.experimental import pallas as pl
from jax.experimental.pallas import tpu as pltpu
from jax.sharding import Mesh, PartitionSpec as P

SEQ_LEN = 1024
TOKENS = 16384
ORDER = 64
HIGHEST = lax.Precision.HIGHEST
F32 = jnp.float32
BF16 = jnp.bfloat16
ANY = pl.BlockSpec(memory_space=pl.ANY)
SMEM = pl.BlockSpec(memory_space=pltpu.SMEM)
VMEM = pl.BlockSpec(memory_space=pltpu.VMEM)
PARAMS = pltpu.CompilerParams(vmem_limit_bytes=14 * 1024 * 1024)
TAIL = 48
NT = (((1,), (1,)), ((), ()))


def swap(size, bit):
    return [(i, i ^ bit) for i in range(size)]


CROSS = [(0, 3), (3, 0), (1, 2), (2, 1)]


def opposed(by):
    return [(i * 2 + k, (i + (by if k == 0 else -by)) % 4 * 2 + k) for i in range(4) for k in range(2)]


def add_over(value, axis, *perms):
    for perm in perms:
        value = value + lax.ppermute(value, axis, perm)
    return value


def after(value, *gates):
    return lax.optimization_barrier((value, *gates))[0] if gates else value


def ring_gather(own, axis):
    held = [own]
    for _ in range(3):
        held.append(lax.ppermute(held[-1], (axis, "c"), opposed(1)))
    return held


def load_kernel(at, weight, evals, out, sems):
    n = weight.shape[0]
    column = pl.multiple_of(at[5], 128)
    copies = [pltpu.make_async_copy(weight, out.at[pl.ds(0, n)], sems.at[0])]
    for i in range(3):
        copies.append(
            pltpu.make_async_copy(
                evals.at[:, pl.ds(column + i * 128, 128)],
                out.at[pl.ds(n, 32), pl.ds(i * 128, 128)],
                sems.at[i + 1],
            )
        )
    for i in range(2):
        copies.append(
            pltpu.make_async_copy(
                evals.at[pl.ds(i * 16, 16), pl.ds(column + 384, 128)],
                out.at[pl.ds(n + 32, 16), pl.ds(i * 128, 128)],
                sems.at[i + 4],
            )
        )
    for copy in copies:
        copy.start()
    for copy in copies:
        copy.wait()


def unload(at, units, pieces, out):
    n = pieces[0].shape[0] - TAIL
    zl, x, c = at[0], at[1], at[4]
    for (s, i), piece in zip(units, pieces):
        row = pl.multiple_of(((zl + 4 - s) % 4 * 4 + (x + 4 + i * (2 * c - 1)) % 4) * 32, 32)
        out[pl.ds(row, 32), 0:384] = piece[n : n + 32, :]
        out[pl.ds(row, 16), 384:512] = piece[n + 32 :, 0:128]
        out[pl.ds(row + 16, 16), 384:512] = piece[n + 32 :, 128:256]


def unit_terms(at, units, weights, grads):
    width = weights[0].shape[1]
    hidden = weights[0].shape[0] - TAIL
    for (s, i), weight in zip(units, weights):
        block = (at[0] + 4 - s) % 4 * 4 + (at[1] + 4 + i * (2 * at[4] - 1)) % 4
        columns = pl.ds(pl.multiple_of(block * width, width), width)
        rows = jnp.concatenate([p[:, columns] for p in grads], axis=0)
        yield lax.dot_general(rows, weight[:hidden, :], NT, preferred_element_type=F32)


def add_kernel(units, first, at, *refs):
    n = len(units)
    weights, grads, out = refs[:n], refs[n : n + 8], refs[-1]
    total = None if first else refs[n + 8][...]
    for term in unit_terms(at, units, weights, grads):
        total = term if total is None else total + term
    out[...] = total


def add_units(name, at, units, slabs, grads, acc=None):
    n = len(units)
    hidden, width = slabs[0][0].shape[0] - TAIL, slabs[0][0].shape[1]
    operands = [at] + [slabs[s][i] for s, i in units] + list(grads) + ([] if acc is None else [acc])
    return pl.pallas_call(
        functools.partial(add_kernel, units, acc is None),
        out_shape=jax.ShapeDtypeStruct((512, hidden), F32),
        in_specs=[SMEM] + [VMEM] * (len(operands) - 1),
        out_specs=VMEM,
        compiler_params=PARAMS,
        cost_estimate=pl.CostEstimate(flops=2 * 512 * hidden * n * width, bytes_accessed=5_000_000, transcendentals=0),
        name=name,
    )(*operands)


def unload_kernel(units, at, *refs):
    unload(at, units, refs[:-1], refs[-1])


def last_kernel(units, at, *refs):
    n = len(units)
    weights, refs = refs[:n], refs[n:]
    halves, refs = (refs[:8], refs[8:16]), refs[16:]
    accs, (gate_pre, up_pre, proj_gate, proj_up, evals_in, keep, send, evals) = refs[:2], refs[2:]
    evals[...] = evals_in[...]
    unload(at, units, weights, evals)
    y, zh, c = at[2], at[3], at[4]
    results = []
    for g in range(4):
        dzh, dc = g // 2, g % 2
        core = c ^ dc
        blocks = [((y + 4 + i * (2 * core - 1)) % 4) * 2 + (zh ^ dzh) for i in range(4)]

        def recorded(ref):
            at_rows = [pl.multiple_of((block * 2 + core) * 64, 64) for block in blocks]
            return jnp.concatenate([ref[pl.ds(r, 64), :] for r in at_rows], axis=0).astype(F32)

        total = accs[dzh][dc * 256 : (dc + 1) * 256, :]
        for term in unit_terms(at, units, weights, halves[dzh][dc * 4 : (dc + 1) * 4]):
            total = total + term
        gate_val, up_val = recorded(gate_pre), recorded(up_pre)
        sig = jax.nn.sigmoid(gate_val)
        gate_grad = (total * up_val * sig * (1.0 + gate_val * (1.0 - sig))).astype(BF16)
        up_grad = (total * gate_val * sig).astype(BF16)
        results.append(
            (
                lax.dot_general(gate_grad, proj_gate[...], NT, preferred_element_type=F32),
                lax.dot_general(up_grad, proj_up[...], NT, preferred_element_type=F32),
            )
        )
        if dc == 0:
            continue
        for i in range(4):
            place = pl.multiple_of((y + 4 + i * (2 * c - 1)) % 4 * 128 + (zh ^ dzh) * 64, 64)
            j = (4 - i) % 4
            sides = []
            for m in range(2):
                here, there = results[-2][m][i * 64 : (i + 1) * 64], results[-1][m][j * 64 : (j + 1) * 64]
                left, right = jnp.where(c == 0, here, there), jnp.where(c == 0, there, here)
                sides.append(jnp.concatenate([left, right], axis=1))
            keep[pl.ds(place, 64), :] = jnp.where(c == 0, sides[0], sides[1])
            send[pl.ds(place, 64), :] = jnp.where(c == 0, sides[1], sides[0])


def last_units(at, units, slabs, own, far, acc_own, acc_far, pres, projs, evals):
    operands = [at] + [slabs[s][i] for s, i in units] + [*own, *far, acc_own, acc_far, *pres, *projs, evals]
    return pl.pallas_call(
        functools.partial(last_kernel, units),
        out_shape=(
            jax.ShapeDtypeStruct((SEQ_LEN // 2, 2 * ORDER), F32),
            jax.ShapeDtypeStruct((SEQ_LEN // 2, 2 * ORDER), F32),
            jax.ShapeDtypeStruct(evals.shape, BF16),
        ),
        in_specs=[SMEM] + [VMEM] * (len(operands) - 1),
        out_specs=(VMEM, VMEM, VMEM),
        compiler_params=PARAMS,
        name="last",
    )(*operands)


def product_kernel(at, here, there, own, far, other, other_far, out):
    n = ORDER
    both = here[...] + there[...]

    def ordered(flag, first, second):
        return jnp.where(
            flag == 0, jnp.concatenate([first, second], axis=0), jnp.concatenate([second, first], axis=0)
        )

    in_proj = ordered(
        at[4], ordered(at[3], own[...], far[...]), ordered(at[3], other[...], other_far[...])
    )
    z = jnp.concatenate([jnp.concatenate([both[:, :n], both[:, n:]], axis=0), in_proj], axis=1)
    g = lax.dot_general(z, z, (((0,), (0,)), ((), ())), precision=HIGHEST, preferred_element_type=F32)
    row = lax.broadcasted_iota(jnp.int32, (n, n), 0)
    col = lax.broadcasted_iota(jnp.int32, (n, n), 1)
    in_moment = g[n:, n:]
    in_diag = jnp.sum(jnp.where(row == col, in_moment, 0.0), axis=0, keepdims=True)
    in_diag = jnp.concatenate([jnp.broadcast_to(in_diag, (8, n))] * 2, axis=1)
    moments = jnp.where(row < col, in_moment, g[:n, :n])
    halves = [jnp.concatenate([v[: n // 2], v[n // 2 :]], axis=1) for v in (moments, g[:n, n:])]
    out[...] = jnp.broadcast_to(jnp.concatenate([halves[0], in_diag, halves[1]], axis=0), out.shape)


def score_kernel(at, moments, side, evals, out, inverse):
    n = ORDER
    packed = sum(moments[i] for i in range(16))
    both = jnp.concatenate([packed[: n // 2, :n], packed[: n // 2, n:]], axis=0)
    in_diag = packed[n // 2 : n // 2 + 1, :n]
    row = lax.broadcasted_iota(jnp.int32, (n, 2 * n), 0)
    col = lax.broadcasted_iota(jnp.int32, (n, 2 * n), 1)
    diag = row == col
    lower = (row >= col)[:, :n]
    mirrored = both.T
    moment = jnp.where(lower, both, mirrored)
    in_moment = jnp.where(lower, mirrored, both)
    in_moment = jnp.where(diag[:, :n], jnp.broadcast_to(in_diag, (n, n)), in_moment)
    right = jnp.concatenate([side[:, :n], side[:, n:]], axis=0)
    eye = jnp.where(diag, 1.0, 0.0)[:, :n]

    def damped(m, rhs):
        a = jnp.concatenate([m * (1.0 / TOKENS), rhs], axis=1)
        damping = 0.1 * jnp.sum(jnp.where(diag, a, 0.0)) / n + 1e-06
        return a + jnp.where(diag, damping, 0.0)

    def spread(a, k):
        return [jnp.broadcast_to(a[:, k + j : k + j + 1], a.shape) for j in range(8)]

    def pivot(a, cols, k, j):
        at_row = row == k + j
        inv = 1.0 / cols[j][k + j : k + j + 1, :]

        def eliminate(m):
            scaled = m[k + j : k + j + 1, :] * inv
            return jnp.where(at_row, scaled, m - cols[j] * scaled)

        return eliminate(a), [m if i <= j else eliminate(m) for i, m in enumerate(cols)]

    a0 = damped(in_moment, eye)
    a1 = damped(moment, right)
    for k in range(0, n, 8):
        c0, c1 = spread(a0, k), spread(a1, k)
        for j in range(8):
            a0, c0 = pivot(a0, c0, k, j)
            a1, c1 = pivot(a1, c1, k, j)
    inverse[...] = a0[:, n:]
    mine = inverse[pl.ds(pl.multiple_of((at[2] * 2 + at[3]) * 8, 8), 8), :]
    part = lax.dot_general(
        mine, a1[:, n:], (((1,), (1,)), ((), ())), precision=HIGHEST, preferred_element_type=F32
    ) * (1.0 / (n * math.sqrt(2.0 * SEQ_LEN)))
    flat = jnp.concatenate([part[i : i + 1, :] for i in range(8)], axis=1)
    high = flat.astype(BF16)
    rest = flat - high.astype(F32)
    mid = rest.astype(BF16)
    low = (rest - mid.astype(F32)).astype(BF16)
    three = jnp.concatenate([high, mid, low], axis=0)
    scores = lax.dot_general(three, evals[...], (((1,), (1,)), ((), ())), preferred_element_type=F32)
    out[...] = scores[0:1] + scores[1:2] + scores[2:3]


def per_device(
    layer_in, out_grad, gate_pre, up_pre, down_weight, proj_in, proj_gate, proj_up, eval_sketch
):
    zl, x, y, zh, c = (lax.axis_index(a) for a in ("zl", "x", "y", "zh", "c"))
    part = 2 * ORDER * ORDER // 16
    at = jnp.stack([zl, x, y, zh, c, (c * 8 + y * 2 + zh) * part]).astype(jnp.int32)
    hidden, width = down_weight.shape
    rows = out_grad.shape[0]
    core = swap(2, 1)

    load = pl.pallas_call(
        load_kernel,
        out_shape=jax.ShapeDtypeStruct((hidden + TAIL, width), BF16),
        in_specs=[SMEM, ANY, ANY],
        out_specs=VMEM,
        scratch_shapes=[pltpu.SemaphoreType.DMA((6,))],
        compiler_params=PARAMS,
        name="load",
    )(at, down_weight, eval_sketch)

    def along_z(value, *gates):
        return lax.ppermute(after(value, *gates), "zl", [(i, (i + 1) % 4) for i in range(4)])

    def over_z(value, *gates):
        return lax.ppermute(after(value, *gates), "zh", core)

    def along_x(n, s):
        slabs[s].append(lax.ppermute(after(slabs[s][-1], *steps[-2:-1], *hold), ("x", "c"), opposed(1)))
        steps.append(slabs[s][-1])

    def other_core(pieces, gate):
        return [lax.ppermute(after(p, gate), "c", core) for p in pieces]

    def origins(dcs, dzh, start):
        return [(dc, dzh, i, start) for dc in dcs for i in range(4)]

    gates = []

    def along(axis, held, *more):
        held.append(lax.ppermute(after(held[-1], *more), (axis, "c"), opposed(1)))

    def other_core(pieces, *more):
        return [lax.ppermute(after(p, *more), "c", core) for p in pieces]

    def along_z(value, *more):
        return lax.ppermute(after(value, *more), "zl", [(i, (i + 1) % 4) for i in range(4)])

    in_rows = [jnp.dot(layer_in, proj_in, preferred_element_type=F32)]
    in_rows.append(lax.ppermute(in_rows[0], "zh", core))
    in_rows += [lax.ppermute(r, "c", core) for r in in_rows]

    slabs, own = [[load]], [out_grad]
    slabs.append([along_z(load)])
    slabs.append([along_z(slabs[1][0], *in_rows)])
    far = [lax.ppermute(after(out_grad, slabs[2][0]), "zh", core)]
    slabs.append([along_z(slabs[2][0], far[0])])
    for _ in range(3):
        along("x", slabs[0])
        along("y", own)
    for _ in range(3):
        along("x", slabs[1])
        along("x", slabs[2])
    for _ in range(3):
        along("y", far, own[3])
    own = own + other_core(own, own[3])
    far = far + other_core(far[:2], far[2]) + other_core(far[2:], far[3])
    units = [(s, i) for s in (0, 1) for i in range(4)]
    acc_own = add_units("own0", at, units, slabs, own)
    along("x", slabs[3], acc_own)
    more = [(2, i) for i in range(4)] + [(3, 0)]
    units += more
    acc_own = add_units("own1", at, more, slabs, own, acc_own)
    along("x", slabs[3], acc_own)
    units += [(3, 1)]
    acc_own = add_units("own2", at, [(3, 1)], slabs, own, acc_own)
    along("x", slabs[3], acc_own)
    evals = pl.pallas_call(
        functools.partial(unload_kernel, units),
        out_shape=jax.ShapeDtypeStruct((512, part), BF16),
        in_specs=[SMEM] + [VMEM] * len(units),
        out_specs=VMEM,
        compiler_params=PARAMS,
        name="unload",
    )(at, *(slabs[s][i] for s, i in units))
    acc_far = add_units("far", at, units, slabs, far)
    keep, send, evals = last_units(
        at,
        [(3, 2), (3, 3)],
        slabs,
        own,
        far,
        acc_own,
        acc_far,
        (gate_pre, up_pre),
        (proj_gate.T, proj_up.T),
        evals,
    )

    keep = keep + lax.ppermute(send, "c", core)
    here = jnp.sum(lax.all_to_all(keep.reshape(4, 2 * rows, 2 * ORDER), "y", 0, 0), axis=0)
    there = lax.ppermute(here, "zh", core)
    packed = ORDER // 2 + 8
    q = pl.pallas_call(
        product_kernel,
        out_shape=jax.ShapeDtypeStruct((4, packed + ORDER // 2, 2 * ORDER), F32),
        in_specs=[SMEM] + [VMEM] * 6,
        out_specs=VMEM,
        name="product",
    )(at, here, there, *in_rows)
    q = jnp.sum(lax.all_to_all(q, "y", 0, 0), axis=0)
    moments = q[:packed]
    moments = lax.all_to_all(jnp.broadcast_to(moments, (16, *moments.shape)), ("zl", "x"), 0, 0)
    scores = pl.pallas_call(
        score_kernel,
        out_shape=jax.ShapeDtypeStruct((1, 512), F32),
        in_specs=[SMEM] + [VMEM] * 3,
        out_specs=VMEM,
        scratch_shapes=[pltpu.VMEM((ORDER, ORDER), F32)],
        compiler_params=PARAMS,
        name="score",
    )(at, moments, q[packed:], evals)
    scores = lax.all_to_all(jnp.broadcast_to(scores, (16, *scores.shape)), ("y", "zh", "c"), 0, 0)
    return jnp.sum(scores, axis=0)


def solution(mesh):
    fine = Mesh(mesh.devices.reshape(4, 4, 4, 2, 2), ("zl", "x", "y", "zh", "c"))
    dp, tensor = ("zl", "x"), ("y", "zh", "c")
    placed = (
        P(dp + tensor, None),
        P(dp + tensor, None),
        P(dp, tensor),
        P(dp, tensor),
        P(tensor, dp),
        P(),
        P(tensor, None),
        P(tensor, None),
        P(dp, None),
    )
    return jax.shard_map(
        per_device, mesh=fine, in_specs=placed, out_specs=P(dp, None), check_vma=False
    )
```

```python
import functools
import math

import jax
import jax.numpy as jnp
from jax import lax
from jax.experimental import pallas as pl
from jax.experimental.pallas import tpu as pltpu
from jax.sharding import Mesh, PartitionSpec as P

SEQ_LEN = 1024
TOKENS = 16384
ORDER = 64
HIGHEST = lax.Precision.HIGHEST
F32 = jnp.float32
BF16 = jnp.bfloat16
ANY = pl.BlockSpec(memory_space=pl.ANY)
SMEM = pl.BlockSpec(memory_space=pltpu.SMEM)
VMEM = pl.BlockSpec(memory_space=pltpu.VMEM)
PARAMS = pltpu.CompilerParams(vmem_limit_bytes=14 * 1024 * 1024)
TAIL = 48
NT = (((1,), (1,)), ((), ()))


def swap(size, bit):
    return [(i, i ^ bit) for i in range(size)]


CROSS = [(0, 3), (3, 0), (1, 2), (2, 1)]


def opposed(by):
    return [(i * 2 + k, (i + (by if k == 0 else -by)) % 4 * 2 + k) for i in range(4) for k in range(2)]


def add_over(value, axis, *perms):
    for perm in perms:
        value = value + lax.ppermute(value, axis, perm)
    return value


def after(value, *gates):
    return lax.optimization_barrier((value, *gates))[0] if gates else value


def ring_gather(own, axis):
    held = [own]
    for _ in range(3):
        held.append(lax.ppermute(held[-1], (axis, "c"), opposed(1)))
    return held


def load_kernel(at, weight, evals, out, sems):
    n = weight.shape[0]
    column = pl.multiple_of(at[5], 128)
    copies = [pltpu.make_async_copy(weight, out.at[pl.ds(0, n)], sems.at[0])]
    for i in range(3):
        copies.append(
            pltpu.make_async_copy(
                evals.at[:, pl.ds(column + i * 128, 128)],
                out.at[pl.ds(n, 32), pl.ds(i * 128, 128)],
                sems.at[i + 1],
            )
        )
    for i in range(2):
        copies.append(
            pltpu.make_async_copy(
                evals.at[pl.ds(i * 16, 16), pl.ds(column + 384, 128)],
                out.at[pl.ds(n + 32, 16), pl.ds(i * 128, 128)],
                sems.at[i + 4],
            )
        )
    for copy in copies:
        copy.start()
    for copy in copies:
        copy.wait()


def unload(at, units, pieces, out):
    n = pieces[0].shape[0] - TAIL
    zl, x, c = at[0], at[1], at[4]
    for (s, i), piece in zip(units, pieces):
        row = pl.multiple_of(((zl + 4 - s) % 4 * 4 + (x + 4 + i * (2 * c - 1)) % 4) * 32, 32)
        out[pl.ds(row, 32), 0:384] = piece[n : n + 32, :]
        out[pl.ds(row, 16), 384:512] = piece[n + 32 :, 0:128]
        out[pl.ds(row + 16, 16), 384:512] = piece[n + 32 :, 128:256]


def unit_terms(at, units, weights, grads):
    width = weights[0].shape[1]
    hidden = weights[0].shape[0] - TAIL
    for (s, i), weight in zip(units, weights):
        block = (at[0] + 4 - s) % 4 * 4 + (at[1] + 4 + i * (2 * at[4] - 1)) % 4
        columns = pl.ds(pl.multiple_of(block * width, width), width)
        rows = jnp.concatenate([p[:, columns] for p in grads], axis=0)
        yield lax.dot_general(rows, weight[:hidden, :], NT, preferred_element_type=F32)


def add_kernel(units, first, at, *refs):
    n = len(units)
    weights, grads, out = refs[:n], refs[n : n + 8], refs[-1]
    total = None if first else refs[n + 8][...]
    for term in unit_terms(at, units, weights, grads):
        total = term if total is None else total + term
    out[...] = total


def add_units(name, at, units, slabs, grads, acc=None):
    n = len(units)
    hidden, width = slabs[0][0].shape[0] - TAIL, slabs[0][0].shape[1]
    operands = [at] + [slabs[s][i] for s, i in units] + list(grads) + ([] if acc is None else [acc])
    return pl.pallas_call(
        functools.partial(add_kernel, units, acc is None),
        out_shape=jax.ShapeDtypeStruct((512, hidden), F32),
        in_specs=[SMEM] + [VMEM] * (len(operands) - 1),
        out_specs=VMEM,
        compiler_params=PARAMS,
        cost_estimate=pl.CostEstimate(flops=2 * 512 * hidden * n * width, bytes_accessed=5_000_000, transcendentals=0),
        name=name,
    )(*operands)


def unload_kernel(units, at, *refs):
    unload(at, units, refs[:-1], refs[-1])


def last_kernel(units, at, *refs):
    n = len(units)
    weights, refs = refs[:n], refs[n:]
    halves, refs = (refs[:8], refs[8:16]), refs[16:]
    accs, (gate_pre, up_pre, proj_gate, proj_up, evals_in, keep, send, evals) = refs[:2], refs[2:]
    evals[...] = evals_in[...]
    unload(at, units, weights, evals)
    y, zh, c = at[2], at[3], at[4]
    results = []
    for g in range(4):
        dzh, dc = g // 2, g % 2
        core = c ^ dc
        blocks = [((y + 4 + i * (2 * core - 1)) % 4) * 2 + (zh ^ dzh) for i in range(4)]

        def recorded(ref):
            at_rows = [pl.multiple_of((block * 2 + core) * 64, 64) for block in blocks]
            return jnp.concatenate([ref[pl.ds(r, 64), :] for r in at_rows], axis=0).astype(F32)

        total = accs[dzh][dc * 256 : (dc + 1) * 256, :]
        for term in unit_terms(at, units, weights, halves[dzh][dc * 4 : (dc + 1) * 4]):
            total = total + term
        gate_val, up_val = recorded(gate_pre), recorded(up_pre)
        sig = jax.nn.sigmoid(gate_val)
        gate_grad = (total * up_val * sig * (1.0 + gate_val * (1.0 - sig))).astype(BF16)
        up_grad = (total * gate_val * sig).astype(BF16)
        results.append(
            (
                lax.dot_general(gate_grad, proj_gate[...], NT, preferred_element_type=F32),
                lax.dot_general(up_grad, proj_up[...], NT, preferred_element_type=F32),
            )
        )
        if dc == 0:
            continue
        for i in range(4):
            place = pl.multiple_of((y + 4 + i * (2 * c - 1)) % 4 * 128 + (zh ^ dzh) * 64, 64)
            j = (4 - i) % 4
            sides = []
            for m in range(2):
                here, there = results[-2][m][i * 64 : (i + 1) * 64], results[-1][m][j * 64 : (j + 1) * 64]
                left, right = jnp.where(c == 0, here, there), jnp.where(c == 0, there, here)
                sides.append(jnp.concatenate([left, right], axis=1))
            keep[pl.ds(place, 64), :] = jnp.where(c == 0, sides[0], sides[1])
            send[pl.ds(place, 64), :] = jnp.where(c == 0, sides[1], sides[0])


def last_units(at, units, slabs, own, far, acc_own, acc_far, pres, projs, evals):
    operands = [at] + [slabs[s][i] for s, i in units] + [*own, *far, acc_own, acc_far, *pres, *projs, evals]
    return pl.pallas_call(
        functools.partial(last_kernel, units),
        out_shape=(
            jax.ShapeDtypeStruct((SEQ_LEN // 2, 2 * ORDER), F32),
            jax.ShapeDtypeStruct((SEQ_LEN // 2, 2 * ORDER), F32),
            jax.ShapeDtypeStruct(evals.shape, BF16),
        ),
        in_specs=[SMEM] + [VMEM] * (len(operands) - 1),
        out_specs=(VMEM, VMEM, VMEM),
        compiler_params=PARAMS,
        name="last",
    )(*operands)


def product_kernel(at, here, there, own, far, other, other_far, out):
    n = ORDER
    both = here[...] + there[...]

    def ordered(flag, first, second):
        return jnp.where(
            flag == 0, jnp.concatenate([first, second], axis=0), jnp.concatenate([second, first], axis=0)
        )

    in_proj = ordered(
        at[4], ordered(at[3], own[...], far[...]), ordered(at[3], other[...], other_far[...])
    )
    z = jnp.concatenate([jnp.concatenate([both[:, :n], both[:, n:]], axis=0), in_proj], axis=1)
    g = lax.dot_general(z, z, (((0,), (0,)), ((), ())), precision=HIGHEST, preferred_element_type=F32)
    row = lax.broadcasted_iota(jnp.int32, (n, n), 0)
    col = lax.broadcasted_iota(jnp.int32, (n, n), 1)
    in_moment = g[n:, n:]
    in_diag = jnp.sum(jnp.where(row == col, in_moment, 0.0), axis=0, keepdims=True)
    in_diag = jnp.concatenate([jnp.broadcast_to(in_diag, (8, n))] * 2, axis=1)
    moments = jnp.where(row < col, in_moment, g[:n, :n])
    halves = [jnp.concatenate([v[: n // 2], v[n // 2 :]], axis=1) for v in (moments, g[:n, n:])]
    out[...] = jnp.broadcast_to(jnp.concatenate([halves[0], in_diag, halves[1]], axis=0), out.shape)


def score_kernel(at, moments, side, evals, out, inverse):
    n = ORDER
    packed = sum(moments[i] for i in range(16))
    both = jnp.concatenate([packed[: n // 2, :n], packed[: n // 2, n:]], axis=0)
    in_diag = packed[n // 2 : n // 2 + 1, :n]
    row = lax.broadcasted_iota(jnp.int32, (n, 2 * n), 0)
    col = lax.broadcasted_iota(jnp.int32, (n, 2 * n), 1)
    diag = row == col
    lower = (row >= col)[:, :n]
    mirrored = both.T
    moment = jnp.where(lower, both, mirrored)
    in_moment = jnp.where(lower, mirrored, both)
    in_moment = jnp.where(diag[:, :n], jnp.broadcast_to(in_diag, (n, n)), in_moment)
    right = jnp.concatenate([side[:, :n], side[:, n:]], axis=0)
    eye = jnp.where(diag, 1.0, 0.0)[:, :n]

    def damped(m, rhs):
        a = jnp.concatenate([m * (1.0 / TOKENS), rhs], axis=1)
        damping = 0.1 * jnp.sum(jnp.where(diag, a, 0.0)) / n + 1e-06
        return a + jnp.where(diag, damping, 0.0)

    def spread(a, k):
        return [jnp.broadcast_to(a[:, k + j : k + j + 1], a.shape) for j in range(8)]

    def pivot(a, cols, k, j):
        at_row = row == k + j
        inv = 1.0 / cols[j][k + j : k + j + 1, :]

        def eliminate(m):
            scaled = m[k + j : k + j + 1, :] * inv
            return jnp.where(at_row, scaled, m - cols[j] * scaled)

        return eliminate(a), [m if i <= j else eliminate(m) for i, m in enumerate(cols)]

    a0 = damped(in_moment, eye)
    a1 = damped(moment, right)
    for k in range(0, n, 8):
        c0, c1 = spread(a0, k), spread(a1, k)
        for j in range(8):
            a0, c0 = pivot(a0, c0, k, j)
            a1, c1 = pivot(a1, c1, k, j)
    inverse[...] = a0[:, n:]
    mine = inverse[pl.ds(pl.multiple_of((at[2] * 2 + at[3]) * 8, 8), 8), :]
    part = lax.dot_general(
        mine, a1[:, n:], (((1,), (1,)), ((), ())), precision=HIGHEST, preferred_element_type=F32
    ) * (1.0 / (n * math.sqrt(2.0 * SEQ_LEN)))
    flat = jnp.concatenate([part[i : i + 1, :] for i in range(8)], axis=1)
    high = flat.astype(BF16)
    rest = flat - high.astype(F32)
    mid = rest.astype(BF16)
    low = (rest - mid.astype(F32)).astype(BF16)
    three = jnp.concatenate([high, mid, low], axis=0)
    scores = lax.dot_general(three, evals[...], (((1,), (1,)), ((), ())), preferred_element_type=F32)
    out[...] = scores[0:1] + scores[1:2] + scores[2:3]


def per_device(
    layer_in, out_grad, gate_pre, up_pre, down_weight, proj_in, proj_gate, proj_up, eval_sketch
):
    zl, x, y, zh, c = (lax.axis_index(a) for a in ("zl", "x", "y", "zh", "c"))
    part = 2 * ORDER * ORDER // 16
    at = jnp.stack([zl, x, y, zh, c, (c * 8 + y * 2 + zh) * part]).astype(jnp.int32)
    hidden, width = down_weight.shape
    rows = out_grad.shape[0]
    core = swap(2, 1)

    load = pl.pallas_call(
        load_kernel,
        out_shape=jax.ShapeDtypeStruct((hidden + TAIL, width), BF16),
        in_specs=[SMEM, ANY, ANY],
        out_specs=VMEM,
        scratch_shapes=[pltpu.SemaphoreType.DMA((6,))],
        compiler_params=PARAMS,
        name="load",
    )(at, down_weight, eval_sketch)

    def along_z(value, *gates):
        return lax.ppermute(after(value, *gates), "zl", [(i, (i + 1) % 4) for i in range(4)])

    def over_z(value, *gates):
        return lax.ppermute(after(value, *gates), "zh", core)

    def along_x(n, s):
        slabs[s].append(lax.ppermute(after(slabs[s][-1], *steps[-2:-1], *hold), ("x", "c"), opposed(1)))
        steps.append(slabs[s][-1])

    def other_core(pieces, gate):
        return [lax.ppermute(after(p, gate), "c", core) for p in pieces]

    def origins(dcs, dzh, start):
        return [(dc, dzh, i, start) for dc in dcs for i in range(4)]

    gates = []

    def along(axis, held, *more):
        held.append(lax.ppermute(after(held[-1], *more), (axis, "c"), opposed(1)))

    def other_core(pieces, *more):
        return [lax.ppermute(after(p, *more), "c", core) for p in pieces]

    def along_z(value, *more):
        return lax.ppermute(after(value, *more), "zl", [(i, (i + 1) % 4) for i in range(4)])

    in_rows = [jnp.dot(layer_in, proj_in, preferred_element_type=F32)]
    in_rows.append(lax.ppermute(in_rows[0], "zh", core))
    in_rows += [lax.ppermute(r, "c", core) for r in in_rows]

    slabs, own = [[load]], [out_grad]
    slabs.append([along_z(load)])
    along("x", slabs[0])
    slabs.append([along_z(slabs[1][0], slabs[0][1], *in_rows)])
    far = [lax.ppermute(after(out_grad, slabs[2][0]), "zh", core)]
    slabs.append([along_z(slabs[2][0], far[0])])
    for i in range(3):
        if i:
            along("x", slabs[0])
        along("y", own)
    for _ in range(3):
        along("x", slabs[1])
        along("x", slabs[2])
    for _ in range(3):
        along("y", far, own[3])
    own = own + other_core(own, own[3])
    far = far + other_core(far[:2], far[2]) + other_core(far[2:], far[3])
    units = [(s, i) for s in (0, 1) for i in range(4)]
    acc_own = add_units("own0", at, units, slabs, own)
    along("x", slabs[3], acc_own)
    more = [(2, i) for i in range(4)] + [(3, 0)]
    units += more
    acc_own = add_units("own1", at, more, slabs, own, acc_own)
    along("x", slabs[3], acc_own)
    units += [(3, 1)]
    acc_own = add_units("own2", at, [(3, 1)], slabs, own, acc_own)
    along("x", slabs[3], acc_own)
    evals = pl.pallas_call(
        functools.partial(unload_kernel, units),
        out_shape=jax.ShapeDtypeStruct((512, part), BF16),
        in_specs=[SMEM] + [VMEM] * len(units),
        out_specs=VMEM,
        compiler_params=PARAMS,
        name="unload",
    )(at, *(slabs[s][i] for s, i in units))
    acc_far = add_units("far", at, units, slabs, far)
    keep, send, evals = last_units(
        at,
        [(3, 2), (3, 3)],
        slabs,
        own,
        far,
        acc_own,
        acc_far,
        (gate_pre, up_pre),
        (proj_gate.T, proj_up.T),
        evals,
    )

    keep = keep + lax.ppermute(send, "c", core)
    here = jnp.sum(lax.all_to_all(keep.reshape(4, 2 * rows, 2 * ORDER), "y", 0, 0), axis=0)
    there = lax.ppermute(here, "zh", core)
    packed = ORDER // 2 + 8
    q = pl.pallas_call(
        product_kernel,
        out_shape=jax.ShapeDtypeStruct((4, packed + ORDER // 2, 2 * ORDER), F32),
        in_specs=[SMEM] + [VMEM] * 6,
        out_specs=VMEM,
        name="product",
    )(at, here, there, *in_rows)
    q = jnp.sum(lax.all_to_all(q, "y", 0, 0), axis=0)
    moments = q[:packed]
    moments = lax.all_to_all(jnp.broadcast_to(moments, (16, *moments.shape)), ("zl", "x"), 0, 0)
    scores = pl.pallas_call(
        score_kernel,
        out_shape=jax.ShapeDtypeStruct((1, 512), F32),
        in_specs=[SMEM] + [VMEM] * 3,
        out_specs=VMEM,
        scratch_shapes=[pltpu.VMEM((ORDER, ORDER), F32)],
        compiler_params=PARAMS,
        name="score",
    )(at, moments, q[packed:], evals)
    scores = lax.all_to_all(jnp.broadcast_to(scores, (16, *scores.shape)), ("y", "zh", "c"), 0, 0)
    return jnp.sum(scores, axis=0)


def solution(mesh):
    fine = Mesh(mesh.devices.reshape(4, 4, 4, 2, 2), ("zl", "x", "y", "zh", "c"))
    dp, tensor = ("zl", "x"), ("y", "zh", "c")
    placed = (
        P(dp + tensor, None),
        P(dp + tensor, None),
        P(dp, tensor),
        P(dp, tensor),
        P(tensor, dp),
        P(),
        P(tensor, None),
        P(tensor, None),
        P(dp, None),
    )
    return jax.shard_map(
        per_device, mesh=fine, in_specs=placed, out_specs=P(dp, None), check_vma=False
    )
```
